256 devices in a mesh: row: 16 (over y, x_hi, core), col: 16 (over z, x_lo).
Axes of the slice: x: 4 (x_hi: 2, x_lo: 2; x = x_hi * 2 + x_lo), y: 4, z: 8, core: 2. Of those that a mesh axis runs over, the one named last changes fastest.
Arguments:
- observed: float32 [8192, 16384], P('row', 'col'), may hold values from -6 to 6
- mask: int32 [8192, 16384], P('row', 'col'), may hold values 0 or 1
- dual: float32 [8192, 16384], P('row', 'col'), may hold values from -0.1 to 0.9
- row_factor: float32 [8192, 128], P(('row', 'col')), may hold values from -1.75 to 1.75
- col_factor: float32 [16384, 128], P(('col', 'row')), may hold values from -1.75 to 1.75
Outputs:
- row_out: float32 [8192, 128], P(('row', 'col'))
- col_out: float32 [16384, 128], P(('col', 'row'))
- dual_out: float32 [8192, 16384], P('row', 'col')
The draws below stay inside these ranges and needn't reach their ends.
All inputs are finite; a program needn't handle non-finite values. No bound on the sum of `mask` on one device may be relied on, other than what follows from the above.
Results may differ from the reference program's by a relative error of at most 0.0001.
Values sent between devices are 32-bit elements; how exact they have to be, the bound alone decides.
A program may use at most 64 MiB of HBM per device.

```python
import jax
import jax.numpy as jnp
from jax import lax

RANK = 128
ITERS = 4
ROWS = 8192
COLS = 16384


def set_ends(drawn, key, least, largest):
    shape = drawn.shape
    index_at = [jax.random.randint(jax.random.fold_in(key, axis), (), 0, shape[axis]) for axis in range(len(shape))]
    drawn = drawn.at[tuple(index_at)].set(least)
    longest = shape.index(max(shape))
    index_at[longest] = (index_at[longest] + 1) % shape[longest]
    return drawn.at[tuple(index_at)].set(largest)


def levels(own_key, extent, pieces, smallest, high):
    factor_of, own = 1.0, jax.random.fold_in(own_key, 6)
    for position, shards_of in pieces:
        steps = jnp.exp(jax.random.uniform(jax.random.fold_in(own, position), (shards_of,), jnp.float32, smallest / len(pieces), high / len(pieces)))
        factor_of = factor_of * jnp.repeat(steps, extent[position] // shards_of).reshape([-1 if axis == position else 1 for axis in range(len(extent))])
    return factor_of


def gaussian(own_key, shape, deviation, bound, split=(), kind=jnp.bfloat16):
    result = deviation * jax.random.normal(own_key, shape, jnp.float32)
    if split:
        result = result * levels(own_key, shape, split, -0.22, 0.18)
    return jnp.clip(result, -bound, bound).astype(kind)


def setup_inputs(seed: int = 0) -> dict:
    splits = jax.random.split(jax.random.key(seed), 6)
    return {
        "observed": gaussian(splits[0], (ROWS, COLS), 1.0, 6.0, ((0, 16), (1, 16)), jnp.float32),
        "mask": set_ends((jax.random.randint(splits[1], (ROWS, COLS), 0, 2) < 1).astype(jnp.int32), jax.random.fold_in(splits[1], 1), 0, 1),
        "dual": jnp.clip(-0.1 + 1 * jax.random.uniform(splits[2], (ROWS, COLS), jnp.float32) ** levels(splits[2], (ROWS, COLS), ((0, 16), (1, 16)), -0.2, 0.2), -0.1, 0.9),
        "row_factor": gaussian(splits[3], (ROWS, RANK), 0.3, 1.75, ((0, 256),), jnp.float32),
        "col_factor": gaussian(splits[4], (COLS, RANK), 0.3, 1.75, ((0, 256),), jnp.float32),
    }


tau_level = 0.9
rho_penalty = 1.0
lam_reg = 0.1
eta_step = 0.05
eps_norm = 1e-06

def reference(observed, mask, dual, row_factor, col_factor):
    maskf = mask.astype(jnp.float32)
    count = (observed.shape[0] + observed.shape[1]) * row_factor.shape[1]
    upper = row_factor
    lower = col_factor
    state = dual
    for sweep in range(ITERS):
        pred = jnp.dot(upper, lower.T, precision=lax.Precision.HIGHEST, preferred_element_type=jnp.float32)
        wide = observed - pred + state / rho_penalty
        clipped = maskf * jnp.clip(wide, -(1.0 - tau_level) / rho_penalty, tau_level / rho_penalty)
        grad_u = -rho_penalty * jnp.dot(clipped, lower, precision=lax.Precision.HIGHEST, preferred_element_type=jnp.float32) + lam_reg * upper
        grad_v = -rho_penalty * jnp.dot(clipped.T, upper, precision=lax.Precision.HIGHEST, preferred_element_type=jnp.float32) + lam_reg * lower
        total = jnp.sum(grad_u * grad_u) + jnp.sum(grad_v * grad_v)
        scale = jnp.sqrt(total / count + eps_norm)
        upper = upper - eta_step * grad_u / scale
        lower = lower - eta_step * grad_v / scale
        state = jnp.where(mask == 1, rho_penalty * clipped, state)
    return (upper, lower, state)
```

```python
import jax
import jax.numpy as jnp
from jax import lax
from jax.experimental import pallas as pl
from jax.experimental.pallas import tpu as pltpu
from jax.sharding import PartitionSpec as P

ITERS = 4
N = 16
MESH = pl.DeviceIdType.MESH

tau_level = 0.9
rho_penalty = 1.0
lam_reg = 0.1
eta_step = 0.05
eps_norm = 1e-06
LOW = -(1.0 - tau_level) / rho_penalty
HIGH = tau_level / rho_penalty

TILE = 128
F32 = jnp.float32
BF16 = jnp.bfloat16


def split(x):
    hi = x.astype(BF16)
    lo = (x - hi.astype(F32)).astype(BF16)
    return hi, lo


def dot(a, b, dims):
    return lax.dot_general(a, b, (dims, ((), ())), preferred_element_type=F32)


def kernel(count, obs_hbm, mask_hbm, dual_hbm, u0, v0, u_out, v_out, state_hbm,
           obs, mask, state, ub, vb, gub, gvb, ucat, vcat, chi, clo, pu, pv, ru, rv,
           n1, n2, ss, rs, ls):
    row = lax.axis_index("row")
    col = lax.axis_index("col")
    ns, ms = u0.shape[0], v0.shape[0]
    nr, nc = obs.shape
    rank = u0.shape[1]

    loads = [pltpu.make_async_copy(a, b, ls.at[i])
             for i, (a, b) in enumerate(((obs_hbm, obs), (mask_hbm, mask), (dual_hbm, state)))]
    for c in loads:
        c.start()

    def along_col(k):
        return (row, lax.rem(col + k, N))

    def along_row(k):
        return (lax.rem(row + k, N), col)

    bar = pltpu.get_barrier_semaphore()
    for k in range(1, N):
        pl.semaphore_signal(bar, inc=1, device_id=along_col(k), device_id_type=MESH)
        pl.semaphore_signal(bar, inc=1, device_id=along_row(k), device_id_type=MESH)
    pl.semaphore_wait(bar, 2 * (N - 1))

    def send(src, dst, i, to):
        pltpu.make_async_remote_copy(
            src_ref=src, dst_ref=dst, send_sem=ss.at[i], recv_sem=rs.at[i],
            device_id=to, device_id_type=MESH).start()

    def wait(ref, sem):
        pltpu.make_async_copy(ref, ref, sem).wait()

    own_u = pl.ds(pl.multiple_of(col * ns, ns), ns)
    own_v = pl.ds(pl.multiple_of(row * ms, ms), ms)
    most_u = pl.ds(0, (N - 1) * ns)
    most_v = pl.ds(0, (N - 1) * ms)

    for k in range(1, N):
        send(v0, vb.at[own_v], 1, along_row(k))
        send(u0, ub.at[own_u], 0, along_col(k))
    ub[own_u, :] = u0[...]
    vb[own_v, :] = v0[...]
    for c in loads:
        c.wait()
    for i, ref in ((0, ub.at[most_u]), (1, vb.at[most_v])):
        wait(ref, rs.at[i])
        wait(ref, ss.at[i])

    def sweep(t, carry):
        uh, ul = split(ub[...])
        ucat[:, :rank] = uh
        ucat[:, rank:] = ul
        vh, vl = split(vb[...])
        vcat[:, :rank] = vh
        vcat[:, rank:] = vl

        @pl.loop(0, nr // TILE)
        def _(i):
            rows = pl.ds(pl.multiple_of(i * TILE, TILE), TILE)
            a = ucat[rows, :]
            vh = vcat[:, :rank]
            pred = dot(a, jnp.concatenate([vh, vh], axis=1), ((1,), (1,)))
            pred += dot(a[:, :rank], vcat[:, rank:], ((1,), (1,)))
            old = state[rows, :]
            wide = obs[rows, :] - pred + old / rho_penalty
            c = jnp.clip(wide, LOW, HIGH)
            on = mask[rows, :] == 1
            state[rows, :] = jnp.where(on, rho_penalty * c, old)
            hi, lo = split(jnp.where(on, c, 0.0))
            chi[rows, :] = hi
            clo[rows, :] = lo

        @pl.loop(0, nr // TILE)
        def _(i):
            rows = pl.ds(pl.multiple_of(i * TILE, TILE), TILE)
            both = jnp.concatenate([chi[rows, :], clo[rows, :]], axis=0)
            g = dot(both, vcat[...], ((1,), (0,)))
            g = g[:TILE] + g[TILE:]
            pu[rows, :] = -rho_penalty * (g[:, :rank] + g[:, rank:])

        for k in range(1, N):
            to = lax.rem(col + k, N)
            send(pu.at[pl.ds(pl.multiple_of(to * ns, ns), ns)], ru.at[k - 1], 2, along_col(k))

        for j in range(nc // 256):
            cols = slice(j * 256, (j + 1) * 256)
            g = dot(chi[:, cols], ucat[...], ((0,), (0,))) + dot(clo[:, cols], ucat[...], ((0,), (0,)))
            pv[cols, :] = -rho_penalty * (g[:, :rank] + g[:, rank:])

        for k in range(1, N):
            to = lax.rem(row + k, N)
            send(pv.at[pl.ds(pl.multiple_of(to * ms, ms), ms)], rv.at[k - 1], 3, along_row(k))

        last = t == ITERS - 1

        wait(ru, rs.at[2])
        gu = pu[own_u, :] + jnp.sum(ru[...], axis=0) + lam_reg * ub[own_u, :]
        gub[own_u, :] = gu

        @pl.when(jnp.logical_not(last))
        def _():
            for k in range(1, N):
                send(gub.at[own_u], gub.at[own_u], 0, along_col(k))

        wait(rv, rs.at[3])
        gv = pv[own_v, :] + jnp.sum(rv[...], axis=0) + lam_reg * vb[own_v, :]
        gvb[own_v, :] = gv
        part = jnp.sum((gu * gu).reshape(ns // 8, 8, rank), axis=0)
        n1[N - 1] = part + jnp.sum((gv * gv).reshape(ms // 8, 8, rank), axis=0)
        for k in range(1, N):
            send(n1.at[N - 1], n1.at[k - 1], 4, along_col(k))

        @pl.when(jnp.logical_not(last))
        def _():
            for k in range(1, N):
                send(gvb.at[own_v], gvb.at[own_v], 1, along_row(k))

        wait(n1.at[pl.ds(0, N - 1)], rs.at[4])
        n2[N - 1] = jnp.sum(n1[...], axis=0)
        for k in range(1, N):
            send(n2.at[N - 1], n2.at[k - 1], 5, along_row(k))
        wait(n2.at[pl.ds(0, N - 1)], rs.at[5])
        total = jnp.sum(n2[...], axis=(0, 1, 2), keepdims=True)[0]
        scale = jnp.sqrt(total / count + eps_norm)

        @pl.when(jnp.logical_not(last))
        def _():
            for i, ref, g, full in ((0, gub.at[most_u], gub, ub), (1, gvb.at[most_v], gvb, vb)):
                wait(ref, rs.at[i])
                wait(ref, ss.at[i])
                full[...] = full[...] - eta_step * g[...] / scale

        @pl.when(last)
        def _():
            u_out[...] = ub[own_u, :] - eta_step * gub[own_u, :] / scale
            v_out[...] = vb[own_v, :] - eta_step * gvb[own_v, :] / scale

        wait(ru, ss.at[2])
        wait(rv, ss.at[3])
        wait(n1.at[pl.ds(0, N - 1)], ss.at[4])
        wait(n2.at[pl.ds(0, N - 1)], ss.at[5])
        return carry

    lax.fori_loop(0, ITERS, sweep, 0)
    out = pltpu.make_async_copy(state, state_hbm, ls.at[0])
    out.start()
    out.wait()


def shards(observed, mask, dual, row_factor, col_factor):
    nr, nc = observed.shape
    ns, rank = row_factor.shape
    ms = col_factor.shape[0]
    count = (nr + nc) * N * rank

    def body(*refs):
        kernel(count, *refs)

    vmem = pl.BlockSpec(memory_space=pltpu.VMEM)
    hbm = pl.BlockSpec(memory_space=pl.ANY)
    return pl.pallas_call(
        body,
        out_shape=(
            jax.ShapeDtypeStruct((ns, rank), F32),
            jax.ShapeDtypeStruct((ms, rank), F32),
            jax.ShapeDtypeStruct((nr, nc), F32),
        ),
        in_specs=[hbm, hbm, hbm, vmem, vmem],
        out_specs=(vmem, vmem, hbm),
        scratch_shapes=[
            pltpu.VMEM((nr, nc), F32),
            pltpu.VMEM((nr, nc), jnp.int32),
            pltpu.VMEM((nr, nc), F32),
            pltpu.VMEM((nr, rank), F32),
            pltpu.VMEM((nc, rank), F32),
            pltpu.VMEM((nr, rank), F32),
            pltpu.VMEM((nc, rank), F32),
            pltpu.VMEM((nr, 2 * rank), BF16),
            pltpu.VMEM((nc, 2 * rank), BF16),
            pltpu.VMEM((nr, nc), BF16),
            pltpu.VMEM((nr, nc), BF16),
            pltpu.VMEM((nr, rank), F32),
            pltpu.VMEM((nc, rank), F32),
            pltpu.VMEM((N - 1, ns, rank), F32),
            pltpu.VMEM((N - 1, ms, rank), F32),
            pltpu.VMEM((N, 8, rank), F32),
            pltpu.VMEM((N, 8, rank), F32),
            pltpu.SemaphoreType.DMA((6,)),
            pltpu.SemaphoreType.DMA((6,)),
            pltpu.SemaphoreType.DMA((3,)),
        ],
        compiler_params=pltpu.CompilerParams(
            collective_id=0, has_side_effects=True, vmem_limit_bytes=48 * 1024 * 1024
        ),
        cost_estimate=pl.CostEstimate(
            flops=ITERS * 6 * nr * nc * rank, bytes_accessed=16 * nr * nc, transcendentals=0
        ),
        name="admm_sweeps",
    )(observed, mask, dual, row_factor, col_factor)


def solution(mesh):
    in_specs = (
        P("row", "col"),
        P("row", "col"),
        P("row", "col"),
        P(("row", "col"), None),
        P(("col", "row"), None),
    )
    out_specs = (P(("row", "col"), None), P(("col", "row"), None), P("row", "col"))
    return jax.shard_map(shards, mesh=mesh, in_specs=in_specs, out_specs=out_specs, check_vma=False)
```

```python
import jax
import jax.numpy as jnp
from jax import lax
from jax.experimental import pallas as pl
from jax.experimental.pallas import tpu as pltpu
from jax.sharding import PartitionSpec as P

ITERS = 4
N = 16
MESH = pl.DeviceIdType.MESH

tau_level = 0.9
rho_penalty = 1.0
lam_reg = 0.1
eta_step = 0.05
eps_norm = 1e-06
LOW = -(1.0 - tau_level) / rho_penalty
HIGH = tau_level / rho_penalty

TILE = 128
FAR_COL = (9, 8, 7, 6, 10, 5, 11, 4, 12, 3, 13, 2, 14, 1, 15)
FAR_ROW = (10, 8, 6, 11, 7, 9, 5, 14, 12, 2, 4, 3, 13, 15, 1)
FAR_CHIP = ((2, 1), (1, 1), (3, 1), (2, 0), (0, 1), (1, 0), (3, 0))
F32 = jnp.float32
BF16 = jnp.bfloat16


def split(x):
    hi = x.astype(BF16)
    lo = (x - hi.astype(F32)).astype(BF16)
    return hi, lo


def dot(a, b, dims):
    return lax.dot_general(a, b, (dims, ((), ())), preferred_element_type=F32)


def kernel(count, obs_hbm, mask_hbm, dual_hbm, u0, v0, u_out, v_out, state_hbm,
           obs, mask, state, ub, vb, gub, gvb, ucat, vcat, chi, clo, pu, pv, sib, ru, rv,
           nb, load, out, us, ur, vs, vr, fs, fr, pus, pur, bs, br, pvs, pvr, nss, nsr):
    row = lax.axis_index("row")
    col = lax.axis_index("col")
    z, xlo = col // 2, lax.rem(col, 2)
    y, xhi, core = row // 4, lax.rem(row // 2, 2), lax.rem(row, 2)
    chip = row // 2
    nr, nc = obs.shape
    ns, ms = nr // N, nc // N
    rank = ub.shape[1]
    sibling = (row + 1 - 2 * core, col)

    own_u = pl.ds(pl.multiple_of(col * ns, ns), ns)
    loads = [pltpu.make_async_copy(a, b, load.at[i])
             for i, (a, b) in enumerate(((u0, ub.at[own_u]), (v0, vb.at[chip, core]),
                                         (obs_hbm, obs), (mask_hbm, mask), (dual_hbm, state)))]
    for c in loads:
        c.start()

    bar = pltpu.get_barrier_semaphore()
    for k in FAR_COL:
        pl.semaphore_signal(bar, inc=1, device_id=(row, lax.rem(col + k, N)), device_id_type=MESH)
    for k in FAR_ROW:
        pl.semaphore_signal(bar, inc=1, device_id=(lax.rem(row + k, N), col), device_id_type=MESH)
    pl.semaphore_wait(bar, 2 * (N - 1))

    def send(src, dst, ss, rs, to):
        pltpu.make_async_remote_copy(
            src_ref=src, dst_ref=dst, send_sem=ss, recv_sem=rs,
            device_id=to, device_id_type=MESH).start()

    def wait(ref, sem):
        pltpu.make_async_copy(ref, ref, sem).wait()

    def chip_at(dy, dx):
        return lax.rem(y + dy, 4) * 2 + (1 - xhi if dx else xhi)

    def gather_u(dst):
        for k in FAR_COL:
            send(dst.at[own_u], dst.at[own_u], us, ur, (row, lax.rem(col + k, N)))

    def gather_v(dst):
        own = dst.at[chip, core]
        for i, (dy, dx) in enumerate(FAR_CHIP):
            send(own, own, vs, vr.at[i], (chip_at(dy, dx) * 2 + core, col))
        send(own, own, fs, fr, sibling)

    def forward_v(dst):
        for i, (dy, dx) in reversed(list(enumerate(FAR_CHIP))):
            got = dst.at[chip_at(4 - dy, dx), core]
            wait(got, vr.at[i])
            send(got, got, fs, fr, sibling)

    def gathered_u(dst):
        most = dst.at[pl.ds(0, (N - 1) * ns)]
        wait(most, ur)
        wait(most, us)

    def gathered_v(dst):
        wait(dst.at[:, 0], fr)
        wait(dst.at[pl.ds(0, 7), 0], vs)
        wait(dst.at[:, 0], fs)

    loads[0].wait()
    gather_u(ub)
    loads[1].wait()
    gather_v(vb)
    forward_v(vb)
    for c in loads[2:]:
        c.wait()
    gathered_v(vb)
    gathered_u(ub)

    def sweep(t, carry):
        last = t == ITERS - 1
        uh, ul = split(ub[...])
        ucat[:, :rank] = uh
        ucat[:, rank:] = ul
        vh, vl = split(vb[...].reshape(nc, rank))
        vcat[:, :rank] = vh
        vcat[:, rank:] = vl

        for dm in (2, 1, 3, 0):
            m = lax.rem(z // 2 + dm, 4)
            rows = pl.ds(pl.multiple_of(m * TILE, TILE), TILE)
            a = ucat[rows, :]
            vh = vcat[:, :rank]
            pred = dot(a, jnp.concatenate([vh, vh], axis=1), ((1,), (1,)))
            pred += dot(a[:, :rank], vcat[:, rank:], ((1,), (1,)))
            old = state[rows, :]
            wide = obs[rows, :] - pred + old / rho_penalty
            c = jnp.clip(wide, LOW, HIGH)
            on = mask[rows, :] == 1
            state[rows, :] = jnp.where(on, rho_penalty * c, old)
            hi, lo = split(jnp.where(on, c, 0.0))
            chi[rows, :] = hi
            clo[rows, :] = lo
            g = dot(jnp.concatenate([hi, lo], axis=0), vcat[...], ((1,), (0,)))
            g = g[:TILE] + g[TILE:]
            pu[rows, :] = -rho_penalty * (g[:, :rank] + g[:, rank:])
            for i in range(4):
                if dm == 0 and i == 0:
                    continue
                to = 4 * m + lax.rem(lax.rem(col, 4) + i, 4)
                src = pu.at[pl.ds(pl.multiple_of(to * ns, ns), ns)]
                send(src, ru.at[col], pus, pur, (row, to))
        ru[col] = pu[own_u, :]

        @pl.when(last)
        def _():
            pltpu.make_async_copy(state, state_hbm, out).start()

        def part_v(i, dy):
            yy = lax.rem(y + dy, 4)
            cols = pl.ds(pl.multiple_of(yy * 256, 256), 256)
            u = ucat[...]
            g = dot(chi[:, cols], u, ((0,), (0,))) + dot(clo[:, cols], u, ((0,), (0,)))
            g = -rho_penalty * (g[:, :rank] + g[:, rank:])
            for hi in range(2):
                for co in range(2):
                    pv[yy, co, hi] = g[(2 * hi + co) * ms:(2 * hi + co + 1) * ms]
            send(pv.at[yy, 1 - core], sib.at[yy], bs, br.at[i], sibling)

        def send_v(i, dy):
            yy = lax.rem(y + dy, 4)
            wait(sib.at[yy], br.at[i])
            pv[yy, core] = pv[yy, core] + sib[yy]
            for dx in (1, 0):
                if dy == 0 and dx == 0:
                    continue
                ch = chip_at(dy, dx)
                hi = 1 - xhi if dx else xhi
                send(pv.at[yy, core, hi], rv.at[chip], pvs, pvr, (ch * 2 + core, col))

        order = (2, 1, 3, 0)
        for i, dy in enumerate(order):
            part_v(i, dy)
            if i:
                send_v(i - 1, order[i - 1])
        send_v(3, 0)
        rv[chip] = pv[y, core, xhi]

        wait(ru.at[pl.ds(0, N - 1)], pur)
        gu = jnp.sum(ru[...], axis=0) + lam_reg * ub[own_u, :]
        gub[own_u, :] = gu

        @pl.when(jnp.logical_not(last))
        def _():
            gather_u(gub)

        wait(rv.at[pl.ds(0, 7)], pvr)
        gv = jnp.sum(rv[...], axis=0) + lam_reg * vb[chip, core]
        gvb[chip, core] = gv

        @pl.when(jnp.logical_not(last))
        def _():
            gather_v(gvb)

        par = lax.rem(t, 2)
        me = row * N + col
        part = jnp.sum(gu * gu, axis=0, keepdims=True) + jnp.sum(gv * gv, axis=0, keepdims=True)
        mine = nb.at[par, pl.ds(me, 1)]
        nb[par, pl.ds(me, 1), :] = part
        for dz in (4, 3, 5, 2, 6, 1, 7, 0):
            zz = lax.rem(z + dz, 8)

            def one(e, carry):
                xx = lax.rem(xlo + lax.rem(e, 2), 2)
                to = (lax.rem(row + e // 2, N), zz * 2 + xx)
                send(mine, mine, nss, nsr.at[par], to)
                return carry

            lax.fori_loop(0 if dz else 1, 2 * N, one, 0)

        @pl.when(jnp.logical_not(last))
        def _():
            forward_v(gvb)

        wait(nb.at[par, pl.ds(0, N * N - 1)], nsr.at[par])
        total = jnp.sum(nb[par], axis=(0, 1), keepdims=True)
        step = eta_step / jnp.sqrt(total / count + eps_norm)

        @pl.when(jnp.logical_not(last))
        def _():
            gathered_u(gub)
            ub[...] = ub[...] - step * gub[...]
            gathered_v(gvb)
            vb[...] = vb[...] - step * gvb[...]

        @pl.when(last)
        def _():
            u_out[...] = ub[own_u, :] - step * gub[own_u, :]
            v_out[...] = vb[chip, core] - step * gvb[chip, core]
            pltpu.make_async_copy(state, state_hbm, out).wait()

        wait(ru.at[pl.ds(0, N - 1)], pus)
        wait(rv.at[pl.ds(0, 7)], pvs)
        wait(sib, bs)
        wait(nb.at[par, pl.ds(0, N * N - 1)], nss)
        return carry

    lax.fori_loop(0, ITERS, sweep, 0)


def shards(observed, mask, dual, row_factor, col_factor):
    nr, nc = observed.shape
    ns, rank = row_factor.shape
    ms = col_factor.shape[0]
    count = (nr + nc) * N * rank

    def body(*refs):
        kernel(count, *refs)

    vmem = pl.BlockSpec(memory_space=pltpu.VMEM)
    hbm = pl.BlockSpec(memory_space=pl.ANY)
    return pl.pallas_call(
        body,
        out_shape=(
            jax.ShapeDtypeStruct((ns, rank), F32),
            jax.ShapeDtypeStruct((ms, rank), F32),
            jax.ShapeDtypeStruct((nr, nc), F32),
        ),
        in_specs=[hbm] * 5,
        out_specs=(vmem, vmem, hbm),
        scratch_shapes=[
            pltpu.VMEM((nr, nc), F32),
            pltpu.VMEM((nr, nc), jnp.int32),
            pltpu.VMEM((nr, nc), F32),
            pltpu.VMEM((nr, rank), F32),
            pltpu.VMEM((8, 2, ms, rank), F32),
            pltpu.VMEM((nr, rank), F32),
            pltpu.VMEM((8, 2, ms, rank), F32),
            pltpu.VMEM((nr, 2 * rank), BF16),
            pltpu.VMEM((nc, 2 * rank), BF16),
            pltpu.VMEM((nr, nc), BF16),
            pltpu.VMEM((nr, nc), BF16),
            pltpu.VMEM((nr, rank), F32),
            pltpu.VMEM((4, 2, 2, ms, rank), F32),
            pltpu.VMEM((4, 2, ms, rank), F32),
            pltpu.VMEM((N, ns, rank), F32),
            pltpu.VMEM((8, ms, rank), F32),
            pltpu.VMEM((2, N * N, rank), F32),
            pltpu.SemaphoreType.DMA((5,)),
            pltpu.SemaphoreType.DMA,
            pltpu.SemaphoreType.DMA,
            pltpu.SemaphoreType.DMA,
            pltpu.SemaphoreType.DMA,
            pltpu.SemaphoreType.DMA((7,)),
            pltpu.SemaphoreType.DMA,
            pltpu.SemaphoreType.DMA,
            pltpu.SemaphoreType.DMA,
            pltpu.SemaphoreType.DMA,
            pltpu.SemaphoreType.DMA,
            pltpu.SemaphoreType.DMA((4,)),
            pltpu.SemaphoreType.DMA,
            pltpu.SemaphoreType.DMA,
            pltpu.SemaphoreType.DMA,
            pltpu.SemaphoreType.DMA((2,)),
        ],
        compiler_params=pltpu.CompilerParams(
            collective_id=0, has_side_effects=True, vmem_limit_bytes=60 * 1024 * 1024
        ),
        cost_estimate=pl.CostEstimate(
            flops=ITERS * 6 * nr * nc * rank, bytes_accessed=16 * nr * nc, transcendentals=0
        ),
        name="admm_sweeps",
    )(observed, mask, dual, row_factor, col_factor)


def solution(mesh):
    in_specs = (
        P("row", "col"),
        P("row", "col"),
        P("row", "col"),
        P(("row", "col"), None),
        P(("col", "row"), None),
    )
    out_specs = (P(("row", "col"), None), P(("col", "row"), None), P("row", "col"))
    return jax.shard_map(shards, mesh=mesh, in_specs=in_specs, out_specs=out_specs, check_vma=False)
```

```python
import jax
import jax.numpy as jnp
from jax import lax
from jax.experimental import pallas as pl
from jax.experimental.pallas import tpu as pltpu
from jax.sharding import PartitionSpec as P

ITERS = 4
N = 16
MESH = pl.DeviceIdType.MESH

tau_level = 0.9
rho_penalty = 1.0
lam_reg = 0.1
eta_step = 0.05
eps_norm = 1e-06
LOW = -(1.0 - tau_level) / rho_penalty
HIGH = tau_level / rho_penalty

TILE = 128
FAR_COL = (9, 8, 7, 6, 10, 5, 11, 4, 12, 3, 13, 2, 14, 1, 15)
FAR_ROW = (10, 8, 6, 11, 7, 9, 5, 14, 12, 2, 4, 3, 13, 15, 1)
FAR_PLANE = sorted(
    ((dy, dx, dc) for dy in range(4) for dx in range(4) for dc in range(2)),
    key=lambda d: -min(d[0], 4 - d[0]) * 4 - min(d[1], 4 - d[1]) * 4 - d[2],
)
FAR_CHIP = ((2, 1), (1, 1), (3, 1), (2, 0), (0, 1), (1, 0), (3, 0))
F32 = jnp.float32
BF16 = jnp.bfloat16


def split(x):
    hi = x.astype(BF16)
    lo = (x - hi.astype(F32)).astype(BF16)
    return hi, lo


def dot(a, b, dims):
    return lax.dot_general(a, b, (dims, ((), ())), preferred_element_type=F32)


def kernel(count, obs_hbm, mask_hbm, dual_hbm, u0, v0, u_out, v_out, state,
           obs, mask, ub, vb, gub, gvb, ucat, vcat, chi, clo, pu, pv, sib, ru, rv,
           nb, load, us, ur, vs, vr, fs, fr, pus, pur, bs, br, pvs, pvr, nss, nsr):
    row = lax.axis_index("row")
    col = lax.axis_index("col")
    z, xlo = col // 2, lax.rem(col, 2)
    y, xhi, core = row // 4, lax.rem(row // 2, 2), lax.rem(row, 2)
    chip = row // 2
    ys = [lax.rem(y + d, 4) for d in range(4)]
    xs = [(lax.rem(xhi * 2 + xlo + d, 4) // 2, lax.rem(xlo + d, 2)) for d in range(4)]
    cores = (core, 1 - core)
    nr, nc = obs.shape
    ns, ms = nr // N, nc // N
    rank = ub.shape[1]
    sibling = (row + 1 - 2 * core, col)

    own_u = pl.ds(pl.multiple_of(col * ns, ns), ns)
    loads = [pltpu.make_async_copy(a, b, load.at[i])
             for i, (a, b) in enumerate(((u0, ub.at[own_u]), (v0, vb.at[chip, core]),
                                         (obs_hbm, obs), (mask_hbm, mask), (dual_hbm, state)))]
    for c in loads:
        c.start()

    bar = pltpu.get_barrier_semaphore()
    for k in FAR_COL:
        pl.semaphore_signal(bar, inc=1, device_id=(row, lax.rem(col + k, N)), device_id_type=MESH)
    for k in FAR_ROW:
        pl.semaphore_signal(bar, inc=1, device_id=(lax.rem(row + k, N), col), device_id_type=MESH)
    pl.semaphore_wait(bar, 2 * (N - 1))

    def send(src, dst, ss, rs, to):
        pltpu.make_async_remote_copy(
            src_ref=src, dst_ref=dst, send_sem=ss, recv_sem=rs,
            device_id=to, device_id_type=MESH).start()

    def wait(ref, sem):
        pltpu.make_async_copy(ref, ref, sem).wait()

    def chip_at(dy, dx):
        return lax.rem(y + dy, 4) * 2 + (1 - xhi if dx else xhi)

    def gather_u(dst):
        for k in FAR_COL:
            send(dst.at[own_u], dst.at[own_u], us, ur, (row, lax.rem(col + k, N)))

    def gather_v(dst):
        own = dst.at[chip, core]
        for i, (dy, dx) in enumerate(FAR_CHIP):
            send(own, own, vs, vr.at[i], (chip_at(dy, dx) * 2 + core, col))
        send(own, own, fs, fr, sibling)

    def forward_v(dst):
        for i, (dy, dx) in reversed(list(enumerate(FAR_CHIP))):
            got = dst.at[chip_at(4 - dy, dx), core]
            wait(got, vr.at[i])
            send(got, got, fs, fr, sibling)

    def gathered_u(dst):
        most = dst.at[pl.ds(0, (N - 1) * ns)]
        wait(most, ur)
        wait(most, us)

    def gathered_v(dst):
        wait(dst.at[:, 0], fr)
        wait(dst.at[pl.ds(0, 7), 0], vs)
        wait(dst.at[:, 0], fs)

    loads[0].wait()
    gather_u(ub)
    loads[1].wait()
    gather_v(vb)
    forward_v(vb)
    for c in loads[2:]:
        c.wait()
    gathered_v(vb)
    gathered_u(ub)

    def sweep(t, carry):
        last = t == ITERS - 1
        uh, ul = split(ub[...])
        ucat[:, :rank] = uh
        ucat[:, rank:] = ul
        vh, vl = split(vb[...].reshape(nc, rank))
        vcat[:, :rank] = vh
        vcat[:, rank:] = vl

        for dm in (2, 1, 3, 0):
            m = lax.rem(z // 2 + dm, 4)
            rows = pl.ds(pl.multiple_of(m * TILE, TILE), TILE)
            a = ucat[rows, :]
            vh = vcat[:, :rank]
            pred = dot(a, jnp.concatenate([vh, vh], axis=1), ((1,), (1,)))
            pred += dot(a[:, :rank], vcat[:, rank:], ((1,), (1,)))
            old = state[rows, :]
            wide = obs[rows, :] - pred + old / rho_penalty
            c = jnp.clip(wide, LOW, HIGH)
            on = mask[rows, :] == 1
            state[rows, :] = jnp.where(on, rho_penalty * c, old)
            hi, lo = split(jnp.where(on, c, 0.0))
            chi[rows, :] = hi
            clo[rows, :] = lo
            g = dot(jnp.concatenate([hi, lo], axis=0), vcat[...], ((1,), (0,)))
            g = g[:TILE] + g[TILE:]
            pu[rows, :] = -rho_penalty * (g[:, :rank] + g[:, rank:])
            for i in range(4):
                if dm == 0 and i == 0:
                    continue
                to = 4 * m + lax.rem(lax.rem(col, 4) + i, 4)
                src = pu.at[pl.ds(pl.multiple_of(to * ns, ns), ns)]
                send(src, ru.at[col], pus, pur, (row, to))
        ru[col] = pu[own_u, :]

        def part_v(i, dy):
            yy = lax.rem(y + dy, 4)
            cols = pl.ds(pl.multiple_of(yy * 256, 256), 256)
            u = ucat[...]
            g = dot(chi[:, cols], u, ((0,), (0,))) + dot(clo[:, cols], u, ((0,), (0,)))
            g = -rho_penalty * (g[:, :rank] + g[:, rank:])
            for hi in range(2):
                for co in range(2):
                    pv[yy, co, hi] = g[(2 * hi + co) * ms:(2 * hi + co + 1) * ms]
            send(pv.at[yy, 1 - core], sib.at[yy], bs, br.at[i], sibling)

        def send_v(i, dy):
            yy = lax.rem(y + dy, 4)
            wait(sib.at[yy], br.at[i])
            pv[yy, core] = pv[yy, core] + sib[yy]
            for dx in (1, 0):
                if dy == 0 and dx == 0:
                    continue
                ch = chip_at(dy, dx)
                hi = 1 - xhi if dx else xhi
                send(pv.at[yy, core, hi], rv.at[chip], pvs, pvr, (ch * 2 + core, col))

        order = (2, 1, 3, 0)
        for i, dy in enumerate(order):
            part_v(i, dy)
            if i:
                send_v(i - 1, order[i - 1])
        send_v(3, 0)
        rv[chip] = pv[y, core, xhi]

        wait(ru.at[pl.ds(0, N - 1)], pur)
        gu = jnp.sum(ru[...], axis=0) + lam_reg * ub[own_u, :]
        gub[own_u, :] = gu

        @pl.when(jnp.logical_not(last))
        def _():
            gather_u(gub)

        wait(rv.at[pl.ds(0, 7)], pvr)
        gv = jnp.sum(rv[...], axis=0) + lam_reg * vb[chip, core]
        gvb[chip, core] = gv

        @pl.when(jnp.logical_not(last))
        def _():
            gather_v(gvb)

        par = lax.rem(t, 2)
        me = row * N + col
        part = jnp.sum(gu * gu, axis=0, keepdims=True) + jnp.sum(gv * gv, axis=0, keepdims=True)
        mine = nb.at[par, pl.ds(me, 1)]
        nb[par, pl.ds(me, 1), :] = part
        def tell(zz, skip):
            for dy, dx, dc in FAR_PLANE[:len(FAR_PLANE) - skip]:
                send(mine, mine, nss, nsr.at[par],
                     (ys[dy] * 4 + xs[dx][0] * 2 + cores[dc], zz * 2 + xs[dx][1]))

        def layer(i, carry):
            dz = 4 + (i + 1) // 2 * (1 - 2 * lax.rem(i, 2))
            tell(lax.rem(z + dz, 8), 0)
            return carry

        lax.fori_loop(0, 7, layer, 0)
        tell(z, 1)

        @pl.when(jnp.logical_not(last))
        def _():
            forward_v(gvb)

        wait(nb.at[par, pl.ds(0, N * N - 1)], nsr.at[par])
        total = jnp.sum(nb[par], axis=(0, 1), keepdims=True)
        step = eta_step / jnp.sqrt(total / count + eps_norm)

        @pl.when(jnp.logical_not(last))
        def _():
            gathered_u(gub)
            ub[...] = ub[...] - step * gub[...]
            gathered_v(gvb)
            vb[...] = vb[...] - step * gvb[...]

        @pl.when(last)
        def _():
            u_out[...] = ub[own_u, :] - step * gub[own_u, :]
            v_out[...] = vb[chip, core] - step * gvb[chip, core]

        wait(ru.at[pl.ds(0, N - 1)], pus)
        wait(rv.at[pl.ds(0, 7)], pvs)
        wait(sib, bs)
        wait(nb.at[par, pl.ds(0, N * N - 1)], nss)
        return carry

    lax.fori_loop(0, ITERS, sweep, 0)


def hand_out(a0, a1, a2, b0, b1, b2, sem):
    copies = [pltpu.make_async_copy(a, b, sem.at[i])
              for i, (a, b) in enumerate(((a2, b2), (a0, b0), (a1, b1)))]
    for c in copies:
        c.start()
    for c in copies:
        c.wait()


def shards(observed, mask, dual, row_factor, col_factor):
    nr, nc = observed.shape
    ns, rank = row_factor.shape
    ms = col_factor.shape[0]
    count = (nr + nc) * N * rank

    def body(*refs):
        kernel(count, *refs)

    vmem = pl.BlockSpec(memory_space=pltpu.VMEM)
    hbm = pl.BlockSpec(memory_space=pltpu.HBM)
    outs = pl.pallas_call(
        body,
        out_shape=(
            pltpu.VMEM((ns, rank), F32),
            pltpu.VMEM((ms, rank), F32),
            pltpu.VMEM((nr, nc), F32),
        ),
        in_specs=[hbm] * 5,
        out_specs=(vmem, vmem, vmem),
        scratch_shapes=[
            pltpu.VMEM((nr, nc), F32),
            pltpu.VMEM((nr, nc), jnp.int32),
            pltpu.VMEM((nr, rank), F32),
            pltpu.VMEM((8, 2, ms, rank), F32),
            pltpu.VMEM((nr, rank), F32),
            pltpu.VMEM((8, 2, ms, rank), F32),
            pltpu.VMEM((nr, 2 * rank), BF16),
            pltpu.VMEM((nc, 2 * rank), BF16),
            pltpu.VMEM((nr, nc), BF16),
            pltpu.VMEM((nr, nc), BF16),
            pltpu.VMEM((nr, rank), F32),
            pltpu.VMEM((4, 2, 2, ms, rank), F32),
            pltpu.VMEM((4, 2, ms, rank), F32),
            pltpu.VMEM((N, ns, rank), F32),
            pltpu.VMEM((8, ms, rank), F32),
            pltpu.VMEM((2, N * N, rank), F32),
            pltpu.SemaphoreType.DMA((5,)),
            pltpu.SemaphoreType.DMA,
            pltpu.SemaphoreType.DMA,
            pltpu.SemaphoreType.DMA,
            pltpu.SemaphoreType.DMA((7,)),
            pltpu.SemaphoreType.DMA,
            pltpu.SemaphoreType.DMA,
            pltpu.SemaphoreType.DMA,
            pltpu.SemaphoreType.DMA,
            pltpu.SemaphoreType.DMA,
            pltpu.SemaphoreType.DMA((4,)),
            pltpu.SemaphoreType.DMA,
            pltpu.SemaphoreType.DMA,
            pltpu.SemaphoreType.DMA,
            pltpu.SemaphoreType.DMA((2,)),
        ],
        compiler_params=pltpu.CompilerParams(
            collective_id=0, has_side_effects=True, vmem_limit_bytes=58 * 1024 * 1024
        ),
        cost_estimate=pl.CostEstimate(
            flops=ITERS * 6 * nr * nc * rank, bytes_accessed=16 * nr * nc, transcendentals=0
        ),
        name="admm_sweeps",
    )(observed, mask, dual, row_factor, col_factor)
    return outs


def solution(mesh):
    in_specs = (
        P("row", "col"),
        P("row", "col"),
        P("row", "col"),
        P(("row", "col"), None),
        P(("col", "row"), None),
    )
    out_specs = (P(("row", "col"), None), P(("col", "row"), None), P("row", "col"))
    return jax.shard_map(shards, mesh=mesh, in_specs=in_specs, out_specs=out_specs, check_vma=False)
```

```python
import jax
import jax.numpy as jnp
from jax import lax
from jax.experimental import pallas as pl
from jax.experimental.pallas import tpu as pltpu
from jax.sharding import PartitionSpec as P

ITERS = 4
N = 16
MESH = pl.DeviceIdType.MESH

tau_level = 0.9
rho_penalty = 1.0
lam_reg = 0.1
eta_step = 0.05
eps_norm = 1e-06
LOW = -(1.0 - tau_level) / rho_penalty
HIGH = tau_level / rho_penalty

TILE = 128
FAR_COL = (9, 8, 7, 6, 10, 5, 11, 4, 12, 3, 13, 2, 14, 1, 15)
FAR_ROW = (10, 8, 6, 11, 7, 9, 5, 14, 12, 2, 4, 3, 13, 15, 1)
FAR_PLANE = sorted(
    ((dy, dx) for dy in range(4) for dx in range(4)),
    key=lambda d: -min(d[0], 4 - d[0]) - min(d[1], 4 - d[1]),
)
TILES = (2, 1, 3, 0)
FAR_CHIP = ((2, 1), (1, 1), (3, 1), (2, 0), (0, 1), (1, 0), (3, 0))
F32 = jnp.float32
BF16 = jnp.bfloat16


def split(x):
    hi = x.astype(BF16)
    lo = (x - hi.astype(F32)).astype(BF16)
    return hi, lo


def dot(a, b, dims):
    return lax.dot_general(a, b, (dims, ((), ())), preferred_element_type=F32)


def kernel(count, obs_hbm, mask_hbm, dual_hbm, u0, v0, u_out, v_out, state,
           obs, mask, ub, vb, gub, gvb, ucat, vcat, chi, clo, pu, pv, sib, ru, rv,
           pb, nb, pair, load, us, ur, vs, vr, fs, fr, pus, pur, bs, br, pvs, pvr, nss, nsr, cs, cr):
    row = lax.axis_index("row")
    col = lax.axis_index("col")
    z, xlo = col // 2, lax.rem(col, 2)
    y, xhi, core = row // 4, lax.rem(row // 2, 2), lax.rem(row, 2)
    chip = row // 2
    ys = [lax.rem(y + d, 4) for d in range(4)]
    xs = [(lax.rem(xhi * 2 + xlo + d, 4) // 2, lax.rem(xlo + d, 2)) for d in range(4)]
    nr, nc = obs.shape
    ns, ms = nr // N, nc // N
    rank = ub.shape[1]
    sibling = (row + 1 - 2 * core, col)

    own_u = pl.ds(pl.multiple_of(col * ns, ns), ns)
    loads = [pltpu.make_async_copy(a, b, load.at[i])
             for i, (a, b) in enumerate(((u0, ub.at[own_u]), (v0, vb.at[chip, core]),
                                         (obs_hbm, obs), (mask_hbm, mask), (dual_hbm, state)))]
    for c in loads:
        c.start()

    bar = pltpu.get_barrier_semaphore()
    for k in FAR_COL:
        pl.semaphore_signal(bar, inc=1, device_id=(row, lax.rem(col + k, N)), device_id_type=MESH)
    for k in FAR_ROW:
        pl.semaphore_signal(bar, inc=1, device_id=(lax.rem(row + k, N), col), device_id_type=MESH)
    pl.semaphore_wait(bar, 2 * (N - 1))

    def send(src, dst, ss, rs, to):
        pltpu.make_async_remote_copy(
            src_ref=src, dst_ref=dst, send_sem=ss, recv_sem=rs,
            device_id=to, device_id_type=MESH).start()

    def wait(ref, sem):
        pltpu.make_async_copy(ref, ref, sem).wait()

    def chip_at(dy, dx):
        return lax.rem(y + dy, 4) * 2 + (1 - xhi if dx else xhi)

    def gather_u(dst):
        for k in FAR_COL:
            send(dst.at[own_u], dst.at[own_u], us, ur, (row, lax.rem(col + k, N)))

    def gather_v(dst):
        own = dst.at[chip, core]
        for i, (dy, dx) in enumerate(FAR_CHIP):
            send(own, own, vs, vr.at[i], (chip_at(dy, dx) * 2 + core, col))
        send(own, own, fs, fr, sibling)

    def forward_v(dst):
        for i, (dy, dx) in reversed(list(enumerate(FAR_CHIP))):
            got = dst.at[chip_at(4 - dy, dx), core]
            wait(got, vr.at[i])
            send(got, got, fs, fr, sibling)

    def gathered_u(dst):
        most = dst.at[pl.ds(0, (N - 1) * ns)]
        wait(most, ur)
        wait(most, us)

    def gathered_v(dst):
        wait(dst.at[:, 0], fr)
        wait(dst.at[pl.ds(0, 7), 0], vs)
        wait(dst.at[:, 0], fs)

    loads[0].wait()
    gather_u(ub)
    loads[1].wait()
    gather_v(vb)
    forward_v(vb)
    for c in loads[2:]:
        c.wait()
    gathered_v(vb)
    gathered_u(ub)

    def sweep(t, carry):
        last = t == ITERS - 1
        uh, ul = split(ub[...])
        ucat[:, :rank] = uh
        ucat[:, rank:] = ul
        vh, vl = split(vb[...].reshape(nc, rank))
        vcat[:, :rank] = vh
        vcat[:, rank:] = vl

        def tile(dm):
            m = lax.rem(z // 2 + dm, 4)
            return m, pl.ds(pl.multiple_of(m * TILE, TILE), TILE)

        def predict(i):
            a = ucat[tile(TILES[i])[1], :]
            vh = vcat[:, :rank]
            pred = dot(a, jnp.concatenate([vh, vh], axis=1), ((1,), (1,)))
            pb[i % 2] = pred + dot(a[:, :rank], vcat[:, rank:], ((1,), (1,)))

        predict(0)
        for i, dm in enumerate(TILES):
            if i < 3:
                predict(i + 1)
            m, rows = tile(dm)
            old = state[rows, :]
            wide = obs[rows, :] - pb[i % 2] + old / rho_penalty
            c = jnp.clip(wide, LOW, HIGH)
            on = mask[rows, :] == 1
            state[rows, :] = jnp.where(on, rho_penalty * c, old)
            hi, lo = split(jnp.where(on, c, 0.0))
            chi[rows, :] = hi
            clo[rows, :] = lo
            g = dot(jnp.concatenate([hi, lo], axis=0), vcat[...], ((1,), (0,)))
            g = g[:TILE] + g[TILE:]
            pu[rows, :] = -rho_penalty * (g[:, :rank] + g[:, rank:])
            for j in range(4):
                if dm == 0 and j == 0:
                    continue
                to = 4 * m + lax.rem(lax.rem(col, 4) + j, 4)
                src = pu.at[pl.ds(pl.multiple_of(to * ns, ns), ns)]
                send(src, ru.at[col], pus, pur, (row, to))
        ru[col] = pu[own_u, :]

        def part_v(i, dy):
            yy = lax.rem(y + dy, 4)
            cols = pl.ds(pl.multiple_of(yy * 256, 256), 256)
            u = ucat[...]
            g = dot(chi[:, cols], u, ((0,), (0,))) + dot(clo[:, cols], u, ((0,), (0,)))
            g = -rho_penalty * (g[:, :rank] + g[:, rank:])
            for hi in range(2):
                for co in range(2):
                    pv[yy, co, hi] = g[(2 * hi + co) * ms:(2 * hi + co + 1) * ms]
            send(pv.at[yy, 1 - core], sib.at[yy], bs, br.at[i], sibling)

        def send_v(i, dy):
            yy = lax.rem(y + dy, 4)
            wait(sib.at[yy], br.at[i])
            pv[yy, core] = pv[yy, core] + sib[yy]
            for dx in (1, 0):
                if dy == 0 and dx == 0:
                    continue
                ch = chip_at(dy, dx)
                hi = 1 - xhi if dx else xhi
                send(pv.at[yy, core, hi], rv.at[chip], pvs, pvr, (ch * 2 + core, col))

        order = (2, 1, 3, 0)
        for i, dy in enumerate(order):
            part_v(i, dy)
            if i:
                send_v(i - 1, order[i - 1])
        send_v(3, 0)
        rv[chip] = pv[y, core, xhi]

        wait(ru.at[pl.ds(0, N - 1)], pur)
        gu = jnp.sum(ru[...], axis=0) + lam_reg * ub[own_u, :]
        gub[own_u, :] = gu

        @pl.when(jnp.logical_not(last))
        def _():
            gather_u(gub)

        wait(rv.at[pl.ds(0, 7)], pvr)
        gv = jnp.sum(rv[...], axis=0) + lam_reg * vb[chip, core]
        gvb[chip, core] = gv

        @pl.when(jnp.logical_not(last))
        def _():
            gather_v(gvb)

        par = lax.rem(t, 2)
        part = jnp.sum(gu * gu, axis=0, keepdims=True) + jnp.sum(gv * gv, axis=0, keepdims=True)
        pair[0:1, :] = part
        send(pair.at[pl.ds(0, 1)], pair.at[pl.ds(8, 1)], cs, cr, sibling)

        wait(pair.at[pl.ds(0, 1)], cr)
        mine = nb.at[par, pl.ds(chip * N + col, 1)]
        nb[par, pl.ds(chip * N + col, 1), :] = part + pair[8:9, :]

        def tell(zz, skip):
            for dy, dx in FAR_PLANE[:len(FAR_PLANE) - skip]:
                send(mine, mine, nss, nsr.at[par],
                     (ys[dy] * 4 + xs[dx][0] * 2 + core, zz * 2 + xs[dx][1]))

        def layer(i, carry):
            dz = 4 + (i + 1) // 2 * (1 - 2 * lax.rem(i, 2))
            tell(lax.rem(z + dz, 8), 0)
            return carry

        lax.fori_loop(0, 7, layer, 0)
        tell(z, 1)

        @pl.when(jnp.logical_not(last))
        def _():
            forward_v(gvb)

        wait(nb.at[par, pl.ds(0, N * N // 2 - 1)], nsr.at[par])
        total = jnp.sum(nb[par], axis=(0, 1), keepdims=True)
        step = eta_step / jnp.sqrt(total / count + eps_norm)

        @pl.when(jnp.logical_not(last))
        def _():
            gathered_u(gub)
            ub[...] = ub[...] - step * gub[...]
            gathered_v(gvb)
            vb[...] = vb[...] - step * gvb[...]

        @pl.when(last)
        def _():
            u_out[...] = ub[own_u, :] - step * gub[own_u, :]
            v_out[...] = vb[chip, core] - step * gvb[chip, core]

        wait(ru.at[pl.ds(0, N - 1)], pus)
        wait(rv.at[pl.ds(0, 7)], pvs)
        wait(sib, bs)
        wait(pair.at[pl.ds(0, 1)], cs)
        wait(nb.at[par, pl.ds(0, N * N // 2 - 1)], nss)
        return carry

    lax.fori_loop(0, ITERS, sweep, 0)


def hand_out(a0, a1, a2, b0, b1, b2, sem):
    copies = [pltpu.make_async_copy(a, b, sem.at[i])
              for i, (a, b) in enumerate(((a2, b2), (a0, b0), (a1, b1)))]
    for c in copies:
        c.start()
    for c in copies:
        c.wait()


def shards(observed, mask, dual, row_factor, col_factor):
    nr, nc = observed.shape
    ns, rank = row_factor.shape
    ms = col_factor.shape[0]
    count = (nr + nc) * N * rank

    def body(*refs):
        kernel(count, *refs)

    vmem = pl.BlockSpec(memory_space=pltpu.VMEM)
    hbm = pl.BlockSpec(memory_space=pltpu.HBM)
    outs = pl.pallas_call(
        body,
        out_shape=(
            pltpu.VMEM((ns, rank), F32),
            pltpu.VMEM((ms, rank), F32),
            pltpu.VMEM((nr, nc), F32),
        ),
        in_specs=[hbm] * 5,
        out_specs=(vmem, vmem, vmem),
        scratch_shapes=[
            pltpu.VMEM((nr, nc), F32),
            pltpu.VMEM((nr, nc), jnp.int32),
            pltpu.VMEM((nr, rank), F32),
            pltpu.VMEM((8, 2, ms, rank), F32),
            pltpu.VMEM((nr, rank), F32),
            pltpu.VMEM((8, 2, ms, rank), F32),
            pltpu.VMEM((nr, 2 * rank), BF16),
            pltpu.VMEM((nc, 2 * rank), BF16),
            pltpu.VMEM((nr, nc), BF16),
            pltpu.VMEM((nr, nc), BF16),
            pltpu.VMEM((nr, rank), F32),
            pltpu.VMEM((4, 2, 2, ms, rank), F32),
            pltpu.VMEM((4, 2, ms, rank), F32),
            pltpu.VMEM((N, ns, rank), F32),
            pltpu.VMEM((8, ms, rank), F32),
            pltpu.VMEM((2, TILE, nc), F32),
            pltpu.VMEM((2, N * N // 2, rank), F32),
            pltpu.VMEM((16, rank), F32),
            pltpu.SemaphoreType.DMA((5,)),
            pltpu.SemaphoreType.DMA,
            pltpu.SemaphoreType.DMA,
            pltpu.SemaphoreType.DMA,
            pltpu.SemaphoreType.DMA((7,)),
            pltpu.SemaphoreType.DMA,
            pltpu.SemaphoreType.DMA,
            pltpu.SemaphoreType.DMA,
            pltpu.SemaphoreType.DMA,
            pltpu.SemaphoreType.DMA,
            pltpu.SemaphoreType.DMA((4,)),
            pltpu.SemaphoreType.DMA,
            pltpu.SemaphoreType.DMA,
            pltpu.SemaphoreType.DMA,
            pltpu.SemaphoreType.DMA((2,)),
            pltpu.SemaphoreType.DMA,
            pltpu.SemaphoreType.DMA,
        ],
        compiler_params=pltpu.CompilerParams(
            collective_id=0, has_side_effects=True, vmem_limit_bytes=58 * 1024 * 1024
        ),
        cost_estimate=pl.CostEstimate(
            flops=ITERS * 6 * nr * nc * rank, bytes_accessed=16 * nr * nc, transcendentals=0
        ),
        name="admm_sweeps",
    )(observed, mask, dual, row_factor, col_factor)
    outs = [pltpu.with_memory_space_constraint(o, pltpu.VMEM) for o in outs]
    return pl.pallas_call(
        hand_out,
        out_shape=[jax.ShapeDtypeStruct(o.shape, o.dtype) for o in outs],
        in_specs=[vmem] * 3,
        out_specs=[hbm] * 3,
        scratch_shapes=[pltpu.SemaphoreType.DMA((3,))],
        name="hand_out",
    )(*outs)


def solution(mesh):
    in_specs = (
        P("row", "col"),
        P("row", "col"),
        P("row", "col"),
        P(("row", "col"), None),
        P(("col", "row"), None),
    )
    out_specs = (P(("row", "col"), None), P(("col", "row"), None), P("row", "col"))
    return jax.shard_map(shards, mesh=mesh, in_specs=in_specs, out_specs=out_specs, check_vma=False)
```

```python
import jax
import jax.numpy as jnp
from jax import lax
from jax.experimental import pallas as pl
from jax.experimental.pallas import tpu as pltpu
from jax.sharding import PartitionSpec as P

ITERS = 4
N = 16
MESH = pl.DeviceIdType.MESH

tau_level = 0.9
rho_penalty = 1.0
lam_reg = 0.1
eta_step = 0.05
eps_norm = 1e-06
LOW = -(1.0 - tau_level) / rho_penalty
HIGH = tau_level / rho_penalty

TILE = 128
FAR_COL = (9, 8, 7, 6, 10, 5, 11, 4, 12, 3, 13, 2, 14, 1, 15)
FAR_ROW = (10, 8, 6, 11, 7, 9, 5, 14, 12, 2, 4, 3, 13, 15, 1)
FAR_PLANE = sorted(
    ((dy, dx) for dy in range(4) for dx in range(4)),
    key=lambda d: -min(d[0], 4 - d[0]) - min(d[1], 4 - d[1]),
)
TILES = (2, 1, 3, 0)
FAR_CHIP = ((2, 1), (1, 1), (3, 1), (2, 0), (0, 1), (1, 0), (3, 0))
F32 = jnp.float32
BF16 = jnp.bfloat16


def split(x):
    hi = x.astype(BF16)
    lo = (x - hi.astype(F32)).astype(BF16)
    return hi, lo


def dot(a, b, dims):
    return lax.dot_general(a, b, (dims, ((), ())), preferred_element_type=F32)


def kernel(count, obs_hbm, mask_hbm, dual_hbm, u0, v0, u_out, v_out, state,
           obs, mask, ub, vb, gub, gvb, ucat, vcat, chi, clo, pu, pv, sib, ru, rv,
           ut, vt, pb, nb, pair, load, us, ur, vs, vr, fs, fr, pus, pur, bs, br, pvs, pvr, nss, nsr, cs, cr):
    row = lax.axis_index("row")
    col = lax.axis_index("col")
    z, xlo = col // 2, lax.rem(col, 2)
    y, xhi, core = row // 4, lax.rem(row // 2, 2), lax.rem(row, 2)
    chip = row // 2
    ys = [lax.rem(y + d, 4) for d in range(4)]
    xs = [(lax.rem(xhi * 2 + xlo + d, 4) // 2, lax.rem(xlo + d, 2)) for d in range(4)]
    nr, nc = obs.shape
    ns, ms = nr // N, nc // N
    rank = ub.shape[1]
    sibling = (row + 1 - 2 * core, col)

    own_u = pl.ds(pl.multiple_of(col * ns, ns), ns)
    loads = [pltpu.make_async_copy(a, b, load.at[i])
             for i, (a, b) in enumerate(((u0, ub.at[own_u]), (v0, vb.at[chip, core]),
                                         (obs_hbm, obs), (mask_hbm, mask), (dual_hbm, state)))]
    for c in loads:
        c.start()

    bar = pltpu.get_barrier_semaphore()
    for k in FAR_COL:
        pl.semaphore_signal(bar, inc=1, device_id=(row, lax.rem(col + k, N)), device_id_type=MESH)
    for k in FAR_ROW:
        pl.semaphore_signal(bar, inc=1, device_id=(lax.rem(row + k, N), col), device_id_type=MESH)
    pl.semaphore_wait(bar, 2 * (N - 1))

    def send(src, dst, ss, rs, to):
        pltpu.make_async_remote_copy(
            src_ref=src, dst_ref=dst, send_sem=ss, recv_sem=rs,
            device_id=to, device_id_type=MESH).start()

    def wait(ref, sem):
        pltpu.make_async_copy(ref, ref, sem).wait()

    def chip_at(dy, dx):
        return lax.rem(y + dy, 4) * 2 + (1 - xhi if dx else xhi)

    def part_u(i, h):
        return pl.ds(pl.multiple_of(i * ns + h * (ns // 2), ns // 2), ns // 2)

    def gather_u(dst, h):
        own = dst.at[part_u(col, h)]
        for k in FAR_COL:
            send(own, own, us.at[h], ur.at[h], (row, lax.rem(col + k, N)))

    def gather_v(dst):
        own = dst.at[chip, core]
        for i, (dy, dx) in enumerate(FAR_CHIP):
            send(own, own, vs, vr.at[i], (chip_at(dy, dx) * 2 + core, col))
        send(own, own, fs, fr, sibling)

    def forward_v(dst):
        for i, (dy, dx) in reversed(list(enumerate(FAR_CHIP))):
            got = dst.at[chip_at(4 - dy, dx), core]
            wait(got, vr.at[i])
            send(got, got, fs, fr, sibling)

    def gathered_u(dst):
        most = dst.at[pl.ds(0, (N - 1) * ns // 2)]
        for h in range(2):
            wait(most, ur.at[h])
            wait(most, us.at[h])

    def gathered_v(dst):
        wait(dst.at[:, 0], fr)
        wait(dst.at[pl.ds(0, 7), 0], vs)
        wait(dst.at[:, 0], fs)

    loads[0].wait()
    for h in range(2):
        gather_u(ub, h)
    loads[1].wait()
    gather_v(vb)
    forward_v(vb)
    for c in loads[2:]:
        c.wait()
    gathered_v(vb)
    gathered_u(ub)

    def sweep(t, carry):
        last = t == ITERS - 1
        uh, ul = split(ub[...])
        ucat[:, :rank] = uh
        ucat[:, rank:] = ul
        uth, utl = split(ub[...].T)
        ut[:rank] = uth
        ut[rank:] = utl
        vh, vl = split(vb[...].reshape(nc, rank))
        vcat[:, :rank] = vh
        vcat[:, rank:] = vl
        th, tl = split(vb[...].reshape(nc, rank).T)
        vt[:rank] = th
        vt[rank:2 * rank] = th
        vt[2 * rank:] = tl

        def tile(dm):
            m = lax.rem(z // 2 + dm, 4)
            return m, pl.ds(pl.multiple_of(m * TILE, TILE), TILE)

        def predict(i):
            a = ucat[tile(TILES[i])[1], :]
            pb[i % 2] = dot(jnp.concatenate([a, a[:, :rank]], axis=1), vt[...], ((1,), (0,)))

        def scatter_u(to, h):
            send(pu.at[part_u(to, h)], ru.at[col, pl.ds(h * (ns // 2), ns // 2)],
                 pus.at[h], pur.at[h], (row, to))

        predict(0)
        for i, dm in enumerate(TILES):
            if i < 3:
                predict(i + 1)
            m, rows = tile(dm)
            old = state[rows, :]
            wide = obs[rows, :] - pb[i % 2] + old
            c = jnp.clip(wide, LOW, HIGH)
            on = mask[rows, :] == 1
            state[rows, :] = jnp.where(on, c, old)
            hi, lo = split(jnp.where(on, c, 0.0))
            chi[rows, :] = hi
            clo[rows, :] = lo
            g = dot(jnp.concatenate([hi, lo], axis=0), vcat[...], ((1,), (0,)))
            g = g[:TILE] + g[TILE:]
            pu[rows, :] = -(g[:, :rank] + g[:, rank:])
            for j in range(4):
                if dm == 0 and j == 0:
                    continue
                to = 4 * m + lax.rem(lax.rem(col, 4) + j, 4)
                scatter_u(to, 0)
        for k in FAR_COL:
            scatter_u(lax.rem(col + k, N), 1)
        ru[col] = pu[own_u, :]

        def part_v(i, dy):
            yy = lax.rem(y + dy, 4)
            cols = pl.ds(pl.multiple_of(yy * 256, 256), 256)
            g = dot(ut[...], chi[:, cols], ((1,), (0,))) + dot(ut[...], clo[:, cols], ((1,), (0,)))
            g = (-(g[:rank] + g[rank:])).T
            for hi in range(2):
                for co in range(2):
                    pv[yy, co, hi] = g[(2 * hi + co) * ms:(2 * hi + co + 1) * ms]
            send(pv.at[yy, 1 - core], sib.at[yy], bs, br.at[i], sibling)

        def send_v(i, dy):
            yy = lax.rem(y + dy, 4)
            wait(sib.at[yy], br.at[i])
            pv[yy, core] = pv[yy, core] + sib[yy]
            for dx in (1, 0):
                if dy == 0 and dx == 0:
                    continue
                ch = chip_at(dy, dx)
                hi = 1 - xhi if dx else xhi
                send(pv.at[yy, core, hi], rv.at[chip], pvs, pvr, (ch * 2 + core, col))

        order = (2, 1, 3, 0)
        for i, dy in enumerate(order):
            part_v(i, dy)
            if i:
                send_v(i - 1, order[i - 1])
        send_v(3, 0)
        rv[chip] = pv[y, core, xhi]

        squares = jnp.zeros((1, rank), F32)
        for h in range(2):
            rows = slice(h * (ns // 2), (h + 1) * (ns // 2))
            wait(ru.at[pl.ds(0, N - 1), rows], pur.at[h])
            gu = jnp.sum(ru[:, rows, :], axis=0) + lam_reg * ub[part_u(col, h), :]
            gub[part_u(col, h), :] = gu
            squares += jnp.sum(gu * gu, axis=0, keepdims=True)

            @pl.when(jnp.logical_not(last))
            def _():
                gather_u(gub, h)

        wait(rv.at[pl.ds(0, 7)], pvr)
        gv = jnp.sum(rv[...], axis=0) + lam_reg * vb[chip, core]
        gvb[chip, core] = gv

        @pl.when(jnp.logical_not(last))
        def _():
            gather_v(gvb)

        par = lax.rem(t, 2)
        part = squares + jnp.sum(gv * gv, axis=0, keepdims=True)
        pair[0:1, :] = part
        send(pair.at[pl.ds(0, 1)], pair.at[pl.ds(8, 1)], cs, cr, sibling)

        wait(pair.at[pl.ds(0, 1)], cr)
        mine = nb.at[par, pl.ds(chip * N + col, 1)]
        nb[par, pl.ds(chip * N + col, 1), :] = part + pair[8:9, :]

        def tell(zz, skip):
            for dy, dx in FAR_PLANE[:len(FAR_PLANE) - skip]:
                send(mine, mine, nss, nsr.at[par],
                     (ys[dy] * 4 + xs[dx][0] * 2 + core, zz * 2 + xs[dx][1]))

        def layer(i, carry):
            dz = 4 + (i + 1) // 2 * (1 - 2 * lax.rem(i, 2))
            tell(lax.rem(z + dz, 8), 0)
            return carry

        lax.fori_loop(0, 7, layer, 0)
        tell(z, 1)

        @pl.when(jnp.logical_not(last))
        def _():
            forward_v(gvb)

        wait(nb.at[par, pl.ds(0, N * N // 2 - 1)], nsr.at[par])
        total = jnp.sum(nb[par], axis=(0, 1), keepdims=True)
        step = eta_step / jnp.sqrt(total / count + eps_norm)

        @pl.when(jnp.logical_not(last))
        def _():
            gathered_u(gub)
            ub[...] = ub[...] - step * gub[...]
            gathered_v(gvb)
            vb[...] = vb[...] - step * gvb[...]

        @pl.when(last)
        def _():
            u_out[...] = ub[own_u, :] - step * gub[own_u, :]
            v_out[...] = vb[chip, core] - step * gvb[chip, core]

        for h in range(2):
            wait(ru.at[pl.ds(0, N - 1), pl.ds(0, ns // 2)], pus.at[h])
        wait(rv.at[pl.ds(0, 7)], pvs)
        wait(sib, bs)
        wait(pair.at[pl.ds(0, 1)], cs)
        wait(nb.at[par, pl.ds(0, N * N // 2 - 1)], nss)
        return carry

    lax.fori_loop(0, ITERS, sweep, 0)


def hand_out(a0, a1, a2, b0, b1, b2, sem):
    copies = [pltpu.make_async_copy(a, b, sem.at[i])
              for i, (a, b) in enumerate(((a2, b2), (a0, b0), (a1, b1)))]
    for c in copies:
        c.start()
    for c in copies:
        c.wait()


def shards(observed, mask, dual, row_factor, col_factor):
    nr, nc = observed.shape
    ns, rank = row_factor.shape
    ms = col_factor.shape[0]
    count = (nr + nc) * N * rank

    def body(*refs):
        kernel(count, *refs)

    vmem = pl.BlockSpec(memory_space=pltpu.VMEM)
    hbm = pl.BlockSpec(memory_space=pltpu.HBM)
    outs = pl.pallas_call(
        body,
        out_shape=(
            pltpu.VMEM((ns, rank), F32),
            pltpu.VMEM((ms, rank), F32),
            pltpu.VMEM((nr, nc), F32),
        ),
        in_specs=[hbm] * 5,
        out_specs=(vmem, vmem, vmem),
        scratch_shapes=[
            pltpu.VMEM((nr, nc), F32),
            pltpu.VMEM((nr, nc), jnp.int32),
            pltpu.VMEM((nr, rank), F32),
            pltpu.VMEM((8, 2, ms, rank), F32),
            pltpu.VMEM((nr, rank), F32),
            pltpu.VMEM((8, 2, ms, rank), F32),
            pltpu.VMEM((nr, 2 * rank), BF16),
            pltpu.VMEM((nc, 2 * rank), BF16),
            pltpu.VMEM((nr, nc), BF16),
            pltpu.VMEM((nr, nc), BF16),
            pltpu.VMEM((nr, rank), F32),
            pltpu.VMEM((4, 2, 2, ms, rank), F32),
            pltpu.VMEM((4, 2, ms, rank), F32),
            pltpu.VMEM((N, ns, rank), F32),
            pltpu.VMEM((8, ms, rank), F32),
            pltpu.VMEM((2 * rank, nr), BF16),
            pltpu.VMEM((3 * rank, nc), BF16),
            pltpu.VMEM((2, TILE, nc), F32),
            pltpu.VMEM((2, N * N // 2, rank), F32),
            pltpu.VMEM((16, rank), F32),
            pltpu.SemaphoreType.DMA((5,)),
            pltpu.SemaphoreType.DMA((2,)),
            pltpu.SemaphoreType.DMA((2,)),
            pltpu.SemaphoreType.DMA,
            pltpu.SemaphoreType.DMA((7,)),
            pltpu.SemaphoreType.DMA,
            pltpu.SemaphoreType.DMA,
            pltpu.SemaphoreType.DMA((2,)),
            pltpu.SemaphoreType.DMA((2,)),
            pltpu.SemaphoreType.DMA,
            pltpu.SemaphoreType.DMA((4,)),
            pltpu.SemaphoreType.DMA,
            pltpu.SemaphoreType.DMA,
            pltpu.SemaphoreType.DMA,
            pltpu.SemaphoreType.DMA((2,)),
            pltpu.SemaphoreType.DMA,
            pltpu.SemaphoreType.DMA,
        ],
        compiler_params=pltpu.CompilerParams(
            collective_id=0, has_side_effects=True, vmem_limit_bytes=58 * 1024 * 1024
        ),
        cost_estimate=pl.CostEstimate(
            flops=ITERS * 6 * nr * nc * rank, bytes_accessed=16 * nr * nc, transcendentals=0
        ),
        name="admm_sweeps",
    )(observed, mask, dual, row_factor, col_factor)
    outs = [pltpu.with_memory_space_constraint(o, pltpu.VMEM) for o in outs]
    return pl.pallas_call(
        hand_out,
        out_shape=[jax.ShapeDtypeStruct(o.shape, o.dtype) for o in outs],
        in_specs=[vmem] * 3,
        out_specs=[hbm] * 3,
        scratch_shapes=[pltpu.SemaphoreType.DMA((3,))],
        name="hand_out",
    )(*outs)


def solution(mesh):
    in_specs = (
        P("row", "col"),
        P("row", "col"),
        P("row", "col"),
        P(("row", "col"), None),
        P(("col", "row"), None),
    )
    out_specs = (P(("row", "col"), None), P(("col", "row"), None), P("row", "col"))
    return jax.shard_map(shards, mesh=mesh, in_specs=in_specs, out_specs=out_specs, check_vma=False)
```

```python
import jax
import jax.numpy as jnp
from jax import lax
from jax.experimental import pallas as pl
from jax.experimental.pallas import tpu as pltpu
from jax.sharding import PartitionSpec as P

ITERS = 4
N = 16
MESH = pl.DeviceIdType.MESH

tau_level = 0.9
rho_penalty = 1.0
lam_reg = 0.1
eta_step = 0.05
eps_norm = 1e-06
LOW = -(1.0 - tau_level) / rho_penalty
HIGH = tau_level / rho_penalty

TILE = 128
FAR_COL = (9, 8, 7, 6, 10, 5, 11, 4, 12, 3, 13, 2, 14, 1, 15)
FAR_ROW = (10, 8, 6, 11, 7, 9, 5, 14, 12, 2, 4, 3, 13, 15, 1)
FAR_PLANE = sorted(
    ((dy, dx) for dy in range(4) for dx in range(4)),
    key=lambda d: -min(d[0], 4 - d[0]) - min(d[1], 4 - d[1]),
)
TILES = (2, 1, 3, 0)
FAR_CHIP = ((2, 1), (1, 1), (3, 1), (2, 0), (0, 1), (1, 0), (3, 0))
F32 = jnp.float32
BF16 = jnp.bfloat16


def split(x):
    hi = x.astype(BF16)
    lo = (x - hi.astype(F32)).astype(BF16)
    return hi, lo


def dot(a, b, dims):
    return lax.dot_general(a, b, (dims, ((), ())), preferred_element_type=F32)


def kernel(count, obs_hbm, mask_hbm, dual_hbm, u0, v0, u_out, v_out, state,
           obs, mask, ub, vb, gub, gvb, ucat, vcat, chi, clo, pu, pv, sib, ru, rv,
           ut, vt, pb, nb, pair, load, us, ur, vs, vr, fs, fr, pus, pur, bs, br, pvs, pvr, nss, nsr, cs, cr):
    row = lax.axis_index("row")
    col = lax.axis_index("col")
    z, xlo = col // 2, lax.rem(col, 2)
    y, xhi, core = row // 4, lax.rem(row // 2, 2), lax.rem(row, 2)
    chip = row // 2
    ys = [lax.rem(y + d, 4) for d in range(4)]
    xs = [(lax.rem(xhi * 2 + xlo + d, 4) // 2, lax.rem(xlo + d, 2)) for d in range(4)]
    nr, nc = obs.shape
    ns, ms = nr // N, nc // N
    rank = ub.shape[1]
    sibling = (row + 1 - 2 * core, col)

    own_u = pl.ds(pl.multiple_of(col * ns, ns), ns)
    loads = [pltpu.make_async_copy(a, b, load.at[i])
             for i, (a, b) in enumerate(((u0, ub.at[own_u]), (v0, vb.at[chip, core]),
                                         (obs_hbm, obs), (mask_hbm, mask), (dual_hbm, state)))]
    for c in loads:
        c.start()

    bar = pltpu.get_barrier_semaphore()
    for k in FAR_COL:
        pl.semaphore_signal(bar, inc=1, device_id=(row, lax.rem(col + k, N)), device_id_type=MESH)
    for k in FAR_ROW:
        pl.semaphore_signal(bar, inc=1, device_id=(lax.rem(row + k, N), col), device_id_type=MESH)
    pl.semaphore_wait(bar, 2 * (N - 1))

    def send(src, dst, ss, rs, to):
        pltpu.make_async_remote_copy(
            src_ref=src, dst_ref=dst, send_sem=ss, recv_sem=rs,
            device_id=to, device_id_type=MESH).start()

    def wait(ref, sem):
        pltpu.make_async_copy(ref, ref, sem).wait()

    def chip_at(dy, dx):
        return lax.rem(y + dy, 4) * 2 + (1 - xhi if dx else xhi)

    def part_u(i, h):
        return pl.ds(pl.multiple_of(i * ns + h * (ns // 2), ns // 2), ns // 2)

    def gather_u(dst, h):
        own = dst.at[part_u(col, h)]
        for k in FAR_COL:
            send(own, own, us.at[h], ur.at[h], (row, lax.rem(col + k, N)))

    def gather_v(dst):
        own = dst.at[chip, core]
        for i, (dy, dx) in enumerate(FAR_CHIP):
            send(own, own, vs, vr.at[i], (chip_at(dy, dx) * 2 + core, col))
        send(own, own, fs, fr, sibling)

    def forward_v(dst):
        for i, (dy, dx) in reversed(list(enumerate(FAR_CHIP))):
            got = dst.at[chip_at(4 - dy, dx), core]
            wait(got, vr.at[i])
            send(got, got, fs, fr, sibling)

    def gathered_u(dst):
        most = dst.at[pl.ds(0, (N - 1) * ns // 2)]
        for h in range(2):
            wait(most, ur.at[h])
            wait(most, us.at[h])

    def gathered_v(dst):
        wait(dst.at[:, 0], fr)
        wait(dst.at[pl.ds(0, 7), 0], vs)
        wait(dst.at[:, 0], fs)

    loads[0].wait()
    loads[1].wait()
    gather_v(vb)
    for h in range(2):
        gather_u(ub, h)
    forward_v(vb)
    for c in loads[2:]:
        c.wait()
    gathered_v(vb)
    gathered_u(ub)

    def sweep(t, carry):
        last = t == ITERS - 1
        uh, ul = split(ub[...])
        ucat[:, :rank] = uh
        ucat[:, rank:] = ul
        uth, utl = split(ub[...].T)
        ut[:rank] = uth
        ut[rank:] = utl
        vh, vl = split(vb[...].reshape(nc, rank))
        vcat[:, :rank] = vh
        vcat[:, rank:] = vl
        th, tl = split(vb[...].reshape(nc, rank).T)
        vt[:rank] = th
        vt[rank:2 * rank] = th
        vt[2 * rank:] = tl

        def tile(dm):
            m = lax.rem(z // 2 + dm, 4)
            return m, pl.ds(pl.multiple_of(m * TILE, TILE), TILE)

        def predict(i):
            a = ucat[tile(TILES[i])[1], :]
            pb[i % 2] = dot(jnp.concatenate([a, a[:, :rank]], axis=1), vt[...], ((1,), (0,)))

        def scatter_u(to, h):
            send(pu.at[part_u(to, h)], ru.at[col, pl.ds(h * (ns // 2), ns // 2)],
                 pus.at[h], pur.at[h], (row, to))

        predict(0)
        for i, dm in enumerate(TILES):
            if i < 3:
                predict(i + 1)
            m, rows = tile(dm)
            old = state[rows, :]
            wide = obs[rows, :] - pb[i % 2] + old
            c = jnp.clip(wide, LOW, HIGH)
            on = mask[rows, :] == 1
            state[rows, :] = jnp.where(on, c, old)
            hi, lo = split(jnp.where(on, c, 0.0))
            chi[rows, :] = hi
            clo[rows, :] = lo
            g = dot(jnp.concatenate([hi, lo], axis=0), vcat[...], ((1,), (0,)))
            g = g[:TILE] + g[TILE:]
            pu[rows, :] = -(g[:, :rank] + g[:, rank:])
            for j in range(4):
                if dm == 0 and j == 0:
                    continue
                to = 4 * m + lax.rem(lax.rem(col, 4) + j, 4)
                scatter_u(to, 0)
        for k in FAR_COL:
            scatter_u(lax.rem(col + k, N), 1)
        ru[col] = pu[own_u, :]

        def part_v(i, dy):
            yy = lax.rem(y + dy, 4)
            cols = pl.ds(pl.multiple_of(yy * 256, 256), 256)
            g = dot(ut[...], chi[:, cols], ((1,), (0,))) + dot(ut[...], clo[:, cols], ((1,), (0,)))
            g = (-(g[:rank] + g[rank:])).T
            for hi in range(2):
                for co in range(2):
                    pv[yy, co, hi] = g[(2 * hi + co) * ms:(2 * hi + co + 1) * ms]
            send(pv.at[yy, 1 - core], sib.at[yy], bs, br.at[i], sibling)

        def send_v(i, dy):
            yy = lax.rem(y + dy, 4)
            wait(sib.at[yy], br.at[i])
            pv[yy, core] = pv[yy, core] + sib[yy]
            for dx in (1, 0):
                if dy == 0 and dx == 0:
                    continue
                ch = chip_at(dy, dx)
                hi = 1 - xhi if dx else xhi
                send(pv.at[yy, core, hi], rv.at[chip], pvs, pvr, (ch * 2 + core, col))

        order = (2, 1, 3, 0)
        for i, dy in enumerate(order):
            part_v(i, dy)
            if i:
                send_v(i - 1, order[i - 1])
        send_v(3, 0)
        rv[chip] = pv[y, core, xhi]

        squares = jnp.zeros((1, rank), F32)
        for h in range(2):
            rows = slice(h * (ns // 2), (h + 1) * (ns // 2))
            wait(ru.at[pl.ds(0, N - 1), rows], pur.at[h])
            gu = jnp.sum(ru[:, rows, :], axis=0) + lam_reg * ub[part_u(col, h), :]
            gub[part_u(col, h), :] = gu
            squares += jnp.sum(gu * gu, axis=0, keepdims=True)

            @pl.when(jnp.logical_not(last))
            def _():
                gather_u(gub, h)

        wait(rv.at[pl.ds(0, 7)], pvr)
        gv = jnp.sum(rv[...], axis=0) + lam_reg * vb[chip, core]
        gvb[chip, core] = gv

        @pl.when(jnp.logical_not(last))
        def _():
            gather_v(gvb)

        par = lax.rem(t, 2)
        part = squares + jnp.sum(gv * gv, axis=0, keepdims=True)
        pair[0:1, :] = part
        send(pair.at[pl.ds(0, 1)], pair.at[pl.ds(8, 1)], cs, cr, sibling)

        wait(pair.at[pl.ds(0, 1)], cr)
        mine = nb.at[par, pl.ds(chip * N + col, 1)]
        nb[par, pl.ds(chip * N + col, 1), :] = part + pair[8:9, :]

        def tell(zz, skip):
            for dy, dx in FAR_PLANE[:len(FAR_PLANE) - skip]:
                send(mine, mine, nss, nsr.at[par],
                     (ys[dy] * 4 + xs[dx][0] * 2 + core, zz * 2 + xs[dx][1]))

        def layer(i, carry):
            dz = 4 + (i + 1) // 2 * (1 - 2 * lax.rem(i, 2))
            tell(lax.rem(z + dz, 8), 0)
            return carry

        lax.fori_loop(0, 7, layer, 0)
        tell(z, 1)

        @pl.when(jnp.logical_not(last))
        def _():
            forward_v(gvb)

        wait(nb.at[par, pl.ds(0, N * N // 2 - 1)], nsr.at[par])
        total = jnp.sum(nb[par], axis=(0, 1), keepdims=True)
        step = eta_step / jnp.sqrt(total / count + eps_norm)

        @pl.when(jnp.logical_not(last))
        def _():
            gathered_u(gub)
            ub[...] = ub[...] - step * gub[...]
            gathered_v(gvb)
            vb[...] = vb[...] - step * gvb[...]

        @pl.when(last)
        def _():
            u_out[...] = ub[own_u, :] - step * gub[own_u, :]
            v_out[...] = vb[chip, core] - step * gvb[chip, core]

        for h in range(2):
            wait(ru.at[pl.ds(0, N - 1), pl.ds(0, ns // 2)], pus.at[h])
        wait(rv.at[pl.ds(0, 7)], pvs)
        wait(sib, bs)
        wait(pair.at[pl.ds(0, 1)], cs)
        wait(nb.at[par, pl.ds(0, N * N // 2 - 1)], nss)
        return carry

    lax.fori_loop(0, ITERS, sweep, 0)


def hand_out(a0, a1, a2, b0, b1, b2, sem):
    rows = a2.shape[0] // 4
    parts = [(a2.at[pl.ds(i * rows, rows)], b2.at[pl.ds(i * rows, rows)]) for i in range(4)]
    copies = [pltpu.make_async_copy(a, b, sem.at[i])
              for i, (a, b) in enumerate(parts + [(a0, b0), (a1, b1)])]
    for c in copies:
        c.start()
    for c in copies:
        c.wait()


def shards(observed, mask, dual, row_factor, col_factor):
    nr, nc = observed.shape
    ns, rank = row_factor.shape
    ms = col_factor.shape[0]
    count = (nr + nc) * N * rank

    def body(*refs):
        kernel(count, *refs)

    vmem = pl.BlockSpec(memory_space=pltpu.VMEM)
    hbm = pl.BlockSpec(memory_space=pltpu.HBM)
    outs = pl.pallas_call(
        body,
        out_shape=(
            pltpu.VMEM((ns, rank), F32),
            pltpu.VMEM((ms, rank), F32),
            pltpu.VMEM((nr, nc), F32),
        ),
        in_specs=[hbm] * 5,
        out_specs=(vmem, vmem, vmem),
        scratch_shapes=[
            pltpu.VMEM((nr, nc), F32),
            pltpu.VMEM((nr, nc), jnp.int32),
            pltpu.VMEM((nr, rank), F32),
            pltpu.VMEM((8, 2, ms, rank), F32),
            pltpu.VMEM((nr, rank), F32),
            pltpu.VMEM((8, 2, ms, rank), F32),
            pltpu.VMEM((nr, 2 * rank), BF16),
            pltpu.VMEM((nc, 2 * rank), BF16),
            pltpu.VMEM((nr, nc), BF16),
            pltpu.VMEM((nr, nc), BF16),
            pltpu.VMEM((nr, rank), F32),
            pltpu.VMEM((4, 2, 2, ms, rank), F32),
            pltpu.VMEM((4, 2, ms, rank), F32),
            pltpu.VMEM((N, ns, rank), F32),
            pltpu.VMEM((8, ms, rank), F32),
            pltpu.VMEM((2 * rank, nr), BF16),
            pltpu.VMEM((3 * rank, nc), BF16),
            pltpu.VMEM((2, TILE, nc), F32),
            pltpu.VMEM((2, N * N // 2, rank), F32),
            pltpu.VMEM((16, rank), F32),
            pltpu.SemaphoreType.DMA((5,)),
            pltpu.SemaphoreType.DMA((2,)),
            pltpu.SemaphoreType.DMA((2,)),
            pltpu.SemaphoreType.DMA,
            pltpu.SemaphoreType.DMA((7,)),
            pltpu.SemaphoreType.DMA,
            pltpu.SemaphoreType.DMA,
            pltpu.SemaphoreType.DMA((2,)),
            pltpu.SemaphoreType.DMA((2,)),
            pltpu.SemaphoreType.DMA,
            pltpu.SemaphoreType.DMA((4,)),
            pltpu.SemaphoreType.DMA,
            pltpu.SemaphoreType.DMA,
            pltpu.SemaphoreType.DMA,
            pltpu.SemaphoreType.DMA((2,)),
            pltpu.SemaphoreType.DMA,
            pltpu.SemaphoreType.DMA,
        ],
        compiler_params=pltpu.CompilerParams(
            collective_id=0, has_side_effects=True, vmem_limit_bytes=58 * 1024 * 1024
        ),
        cost_estimate=pl.CostEstimate(
            flops=ITERS * 6 * nr * nc * rank, bytes_accessed=16 * nr * nc, transcendentals=0
        ),
        name="admm_sweeps",
    )(observed, mask, dual, row_factor, col_factor)
    outs = [pltpu.with_memory_space_constraint(o, pltpu.VMEM) for o in outs]
    return pl.pallas_call(
        hand_out,
        out_shape=[jax.ShapeDtypeStruct(o.shape, o.dtype) for o in outs],
        in_specs=[vmem] * 3,
        out_specs=[hbm] * 3,
        scratch_shapes=[pltpu.SemaphoreType.DMA((6,))],
        name="hand_out",
    )(*outs)


def solution(mesh):
    in_specs = (
        P("row", "col"),
        P("row", "col"),
        P("row", "col"),
        P(("row", "col"), None),
        P(("col", "row"), None),
    )
    out_specs = (P(("row", "col"), None), P(("col", "row"), None), P("row", "col"))
    return jax.shard_map(shards, mesh=mesh, in_specs=in_specs, out_specs=out_specs, check_vma=False)
```
